32 devices in a mesh: vv: 8 (over z, x), oo: 4 (over y, core).
Axes of the slice: x: 2, y: 2, z: 4, core: 2. Of those that a mesh axis runs over, the one named last changes fastest.
Arguments:
- integrals: bfloat16 [16384, 20480], P('vv', 'oo'), may hold values from -0.0390625 to 0.0390625
- t2: bfloat16 [8, 20480, 1280], P(None, 'oo', 'vv'), may hold values from -6 to 6
- block_owner: int32 [8], replicated, may hold values from 0 to 7, as said below
Outputs:
- residual: float32 [16384, 1280], P('vv', 'oo')
The draws below stay inside these ranges and needn't reach their ends.
Inputs may be any that keep to these rules, and one draw needn't show every extreme that they name: `block_owner`: each pair irrep 0 to 7 is named by exactly 1 row blocks.
All inputs are finite; a program needn't handle non-finite values.
Results may differ from the reference program's by a relative error of at most 0.0003.
Values may be sent and summed in bfloat16 or wider, within the bound.
No kernel may reach another device: no remote copies, remote signals or barrier semaphores. Data moves between devices by JAX's collectives and lax.ppermute only.
A program may use at most 128 MiB of HBM per device.

```python
import jax
import jax.numpy as jnp
from jax import lax

G = 8
DE = 20480
IJ = 1280
ROW_DEV = 2048
OWNERS = 8
ROWS = 16384


def draw_block_owner(key, part):
    labels = jnp.arange(OWNERS, dtype=jnp.int32) % G
    return jax.random.permutation(key, labels).astype(jnp.int32)


def raised(entries, stream_key, source, target, shards_of, factor):
    def block_of(position):
        return (jnp.arange(entries.shape[position]) // (entries.shape[position] // shards_of)).reshape((-1,) + (1,) * (entries.ndim - 1 - position))

    first = jax.random.permutation(stream_key, shards_of)[block_of(target)]
    second = (block_of(target) + shards_of // 2) % shards_of
    return jnp.where((block_of(source) == first) | (block_of(source) == second), factor * entries, entries)


def steps_of(key, extent, cuts, smallest, high):
    loudness = 1.0
    for position, parts in cuts:
        heights = jax.random.uniform(jax.random.fold_in(jax.random.fold_in(key, 6), position), (parts,), jnp.float32, smallest / len(cuts), high / len(cuts))
        loudness = loudness * jnp.repeat(jnp.exp(heights), extent[position] // parts).reshape((-1,) + (1,) * (len(extent) - 1 - position))
    return loudness


def normal_values(key, extent, spread, most, shards=(), held_as=jnp.bfloat16):
    entries = jax.random.normal(key, extent, jnp.float32) * spread
    if len(shards) > 0:
        entries = steps_of(key, extent, shards, -0.22, 0.18) * entries
    return jnp.clip(entries, min=-most, max=most).astype(held_as)


def heavy_noise(stream_key, extent, deviation, reach, split, heavy, kind=jnp.bfloat16):
    entries = deviation * jax.random.normal(stream_key, extent, jnp.float32)
    if split:
        entries = entries * steps_of(stream_key, extent, split, -0.22, 0.18)
    return jnp.clip(raised(entries, jax.random.fold_in(stream_key, 3), *heavy), -reach, reach).astype(kind)


def setup_inputs(seed: int = 0) -> dict:
    seeds = jax.random.split(jax.random.key(seed), 4)
    return {
        "integrals": normal_values(seeds[0], (ROWS, DE), DE ** -0.5, 0.0390625, ((0, 8), (1, 4))),
        "t2": heavy_noise(seeds[1], (G, DE, IJ), 1.0, 6.0, ((1, 4), (2, 8)), (1, 2, 8, 2.0)),
        "block_owner": draw_block_owner(jax.random.fold_in(seeds[3], 71), 0),
    }


def reference(integrals, t2, block_owner):
    blocks = integrals.reshape(OWNERS, ROW_DEV, DE)

    def one_block(pair):
        rows, irrep = pair
        return jnp.dot(rows, t2[irrep], preferred_element_type=jnp.float32)

    result = lax.map(one_block, (blocks, block_owner))
    return result.reshape(OWNERS * ROW_DEV, IJ)
```

```python
import math

import jax
import jax.numpy as jnp
from jax import lax
from jax.experimental import pallas as pl
from jax.experimental.pallas import tpu as pltpu
from jax.sharding import PartitionSpec as P

BLOCK = 512
LINK_SHARE = 64
CUT = 80


def cut_kernel(owner, me, *refs):
    n = len(refs) // 2
    for block, out in zip(refs[:n], refs[n:]):
        out[...] = block[0]


def cut(parts, owner, me, blocks):
    depth = blocks.shape[2]
    _, start, width = parts[0]
    step = math.gcd(math.gcd(start, width), CUT)
    return pl.pallas_call(
        cut_kernel,
        grid_spec=pltpu.PrefetchScalarGridSpec(
            num_scalar_prefetch=2,
            grid=(width // step,),
            in_specs=[
                pl.BlockSpec((1, step, depth), lambda i, owner, me, mask=mask: (owner[me[0] ^ mask], start // step + i, 0))
                for mask, _, _ in parts
            ],
            out_specs=[pl.BlockSpec((step, depth), lambda i, owner, me: (i, 0))] * len(parts),
        ),
        out_shape=[jax.ShapeDtypeStruct((width, depth), blocks.dtype)] * len(parts),
        cost_estimate=pl.CostEstimate(flops=0, bytes_accessed=4 * depth * width * len(parts), transcendentals=0),
        compiler_params=pltpu.CompilerParams(vmem_limit_bytes=56 * 2**20),
    )(owner, me, *[blocks] * len(parts))


def product_kernel(*refs):
    *pieces, rows, out, held = refs

    @pl.when(pl.program_id(0) == 0)
    def _():
        at = 0
        for piece in pieces:
            held[at : at + piece.shape[0], :] = piece[...]
            at += piece.shape[0]

    out[...] = lax.dot_general(held[...], rows[...], (((1,), (1,)), ((), ())), preferred_element_type=jnp.float32)


def product(pieces, integrals):
    depth, rows = pieces[0].shape[1], integrals.shape[0]
    n = sum(piece.shape[0] for piece in pieces)
    block = min(BLOCK, rows)
    return pl.pallas_call(
        product_kernel,
        grid=(rows // block,),
        in_specs=[pl.BlockSpec(piece.shape, lambda i: (0, 0)) for piece in pieces]
        + [pl.BlockSpec((block, depth), lambda i: (i, 0))],
        out_specs=pl.BlockSpec((n, block), lambda i: (0, i)),
        out_shape=jax.ShapeDtypeStruct((n, rows), jnp.float32),
        scratch_shapes=[pltpu.VMEM((n, depth), pieces[0].dtype)],
        cost_estimate=pl.CostEstimate(
            flops=2 * n * depth * rows // LINK_SHARE,
            bytes_accessed=(2 * (n + rows) * depth + 4 * n * rows) // LINK_SHARE,
            transcendentals=0,
        ),
        compiler_params=pltpu.CompilerParams(vmem_limit_bytes=48 * 2**20),
    )(*pieces, integrals)


def after(xs, *others):
    return list(lax.optimization_barrier((*xs, *others))[: len(xs)])


def local(vv, oo, integrals, t2, block_owner):
    v, o = lax.axis_index("vv"), lax.axis_index("oo")
    blocks = jnp.swapaxes(t2, 1, 2)
    columns, rows = blocks.shape[1], integrals.shape[0]
    ratio = vv // oo
    offset = (v // ratio) ^ o
    me = v.reshape(1)
    half, quarter = vv // 2, vv // 4

    top = oo // 2
    bits = [1 << k for k in range(top.bit_length() - 1)]
    whole = {mask: (mask, 0, columns) for mask in range(vv)}
    first = [whole[mask] for mask in [*range(half, half + quarter), *range(1, half)]]
    second = [whole[mask] for mask in range(half + quarter, vv)]
    ready = {}
    for some in (first[:quarter], [*first[quarter:], whole[0], *second]):
        ready.update(zip(some, cut(some, block_owner, me, blocks)))
    got = {whole[0]: ready[whole[0]]}

    def fetch(parts, *before):
        sent = [ready[part] for part in parts]
        for part, x in zip(parts, after(sent, *before) if before else sent):
            got[part] = lax.ppermute(x, "vv", [(i, i ^ part[0]) for i in range(vv)])

    made = []

    def multiply(parts, *before):
        made.append(product(after([got[part] for part in parts], *made[-1:], *before), integrals))
        return made[-1]

    def hop(x, j, bit):
        pairs = [
            (a * oo + b, a * oo + (b ^ bit))
            for a in range(vv)
            for b in range(oo)
            if ((a // ratio) ^ b ^ j) % (2 * bit) == bit
        ]
        return lax.ppermute(x, ("vv", "oo"), pairs)

    def inner(each):
        for part in each:
            for bit in bits:
                each[part] = each[part] + hop(each[part], part[0] // ratio, bit)
        return each

    def outer(each):
        return {part: x + hop(x, part[0] // ratio, top) for part, x in each.items()}

    def fold(x):
        for bit in bits:
            mine = (offset // bit) % 2 == 1
            n = x[0].shape[0]
            sent = jnp.concatenate([jnp.where(mine, one, two) for one, two in zip(x[::2], x[1::2])])
            came = lax.ppermute(sent, "oo", [(i, i ^ bit) for i in range(oo)])
            x = [jnp.where(mine, two, one) + came[i * n : (i + 1) * n] for i, (one, two) in enumerate(zip(x[::2], x[1::2]))]
        return x[0]

    def place(out, x, part, mine):
        row = ((v ^ part[0]) % ratio) * columns + part[1]
        return lax.dynamic_update_slice(out, jnp.where(mine, x, lax.dynamic_slice(out, (row, 0), x.shape)), (row, 0))

    fetch(first)
    fetch(second[:-1], *[got[part] for part in first[:quarter]])
    middle = [got[part] for part in second[:-1]]
    fetch(second[-1:], *middle)
    near = []
    for j in range(top):
        arrived = [got[part] for part in first[: quarter * (j + 1) // top]]
        near.append(multiply([whole[mask] for mask in range(j * ratio, (j + 1) * ratio)], *arrived))
    early = {}
    for j in range(top, top + top // 2):
        early[j * ratio, 0, ratio * columns] = multiply([whole[mask] for mask in range(j * ratio, (j + 1) * ratio)])
    near = fold(near)
    early = inner(dict(zip(early, after(list(early.values()), *middle))))
    pairs = [(a * oo + b, a * oo + (b ^ top)) for a in range(vv) for b in range(oo) if ((a // ratio) ^ b) & top]
    near = near + lax.ppermute(near, ("vv", "oo"), pairs)
    early = outer(early)
    late, before = {}, []
    for part in second:
        if part == second[-1]:
            before += [near, *early.values()]
        sums = inner({part: multiply([part], *before)})
        before = list(sums.values())
        late.update(outer(sums))

    out = jnp.zeros((ratio * columns, rows), jnp.float32)
    for low in range(ratio):
        rows_of = slice(low * columns, (low + 1) * columns)
        out = place(out, near[rows_of], whole[low], offset < top)
        for part, x in early.items():
            out = place(out, x[rows_of], whole[part[0] + low], offset == part[0] // ratio)
    for part, x in late.items():
        out = place(out, x, part, offset == part[0] // ratio)
    return out.T


def solution(mesh):
    vv, oo = mesh.shape["vv"], mesh.shape["oo"]
    in_specs = (P("vv", "oo"), P(None, "oo", "vv"), P())
    return jax.shard_map(
        lambda *a: local(vv, oo, *a), mesh=mesh, in_specs=in_specs, out_specs=P("vv", "oo"), check_vma=False
    )
```

```python
import math

import jax
import jax.numpy as jnp
from jax import lax
from jax.experimental import pallas as pl
from jax.experimental.pallas import tpu as pltpu
from jax.sharding import PartitionSpec as P

BLOCK = 512
SHORT = 10
TILE = 16
LINK_SHARE = 64
CUT = 80


def cut_kernel(owner, me, *refs):
    n = len(refs) // 2
    for block, out in zip(refs[:n], refs[n:]):
        out[...] = block[0]


def cut(parts, owner, me, blocks):
    depth = blocks.shape[2]
    _, start, width = parts[0]
    step = math.gcd(math.gcd(start, width), CUT)
    return pl.pallas_call(
        cut_kernel,
        grid_spec=pltpu.PrefetchScalarGridSpec(
            num_scalar_prefetch=2,
            grid=(width // step,),
            in_specs=[
                pl.BlockSpec((1, step, depth), lambda i, owner, me, mask=mask: (owner[me[0] ^ mask], start // step + i, 0))
                for mask, _, _ in parts
            ],
            out_specs=[pl.BlockSpec((step, depth), lambda i, owner, me: (i, 0))] * len(parts),
        ),
        out_shape=[jax.ShapeDtypeStruct((width, depth), blocks.dtype)] * len(parts),
        cost_estimate=pl.CostEstimate(flops=0, bytes_accessed=4 * depth * width * len(parts), transcendentals=0),
        compiler_params=pltpu.CompilerParams(vmem_limit_bytes=56 * 2**20),
    )(owner, me, *[blocks] * len(parts))


def product_kernel(*refs):
    *pieces, rows, out, held = refs

    @pl.when(pl.program_id(0) == 0)
    def _():
        at = 0
        for piece in pieces:
            held[at : at + piece.shape[0], :] = piece[...]
            at += piece.shape[0]

    out[...] = lax.dot_general(held[...], rows[...], (((1,), (1,)), ((), ())), preferred_element_type=jnp.float32)


def product(pieces, integrals):
    depth, rows = pieces[0].shape[1], integrals.shape[0]
    n = sum(piece.shape[0] for piece in pieces)
    block = min(BLOCK, rows)
    return pl.pallas_call(
        product_kernel,
        grid=(rows // block,),
        in_specs=[pl.BlockSpec(piece.shape, lambda i: (0, 0)) for piece in pieces]
        + [pl.BlockSpec((block, depth), lambda i: (i, 0))],
        out_specs=pl.BlockSpec((n, block), lambda i: (0, i)),
        out_shape=jax.ShapeDtypeStruct((n, rows), jnp.float32),
        scratch_shapes=[pltpu.VMEM((n, depth), pieces[0].dtype)],
        cost_estimate=pl.CostEstimate(
            flops=2 * n * depth * rows // LINK_SHARE,
            bytes_accessed=(2 * (n + rows) * depth + 4 * n * rows) // LINK_SHARE,
            transcendentals=0,
        ),
        compiler_params=pltpu.CompilerParams(vmem_limit_bytes=48 * 2**20),
    )(*pieces, integrals)


def after(xs, *others):
    return list(lax.optimization_barrier((*xs, *others))[: len(xs)])


def local(vv, oo, integrals, t2, block_owner):
    v, o = lax.axis_index("vv"), lax.axis_index("oo")
    blocks = jnp.swapaxes(t2, 1, 2)
    columns, rows = blocks.shape[1], integrals.shape[0]
    ratio = vv // oo
    offset = (v // ratio) ^ o
    me = v.reshape(1)
    half, quarter = vv // 2, vv // 4

    top = oo // 2
    bits = [1 << k for k in range(top.bit_length() - 1)]
    whole = {mask: (mask, 0, columns) for mask in range(vv)}
    first = [whole[mask] for mask in [*range(half, half + quarter), *range(1, half)]]
    short = max(columns // SHORT // TILE, 1) * TILE
    cuts = [0, columns - short, columns]
    third = [(vv - 1, one, two - one) for one, two in zip(cuts, cuts[1:])]
    second = [whole[mask] for mask in range(half + quarter, vv - 1)]
    ready = {}
    for some in (first[:quarter], [*first[quarter:], whole[0], *second, whole[vv - 1]]):
        ready.update(zip(some, cut(some, block_owner, me, blocks)))
    got = {whole[0]: ready[whole[0]]}
    for part in third:
        ready[part] = ready[whole[vv - 1]][part[1] : part[1] + part[2]]

    def fetch(parts, *before):
        sent = [ready[part] for part in parts]
        for part, x in zip(parts, after(sent, *before) if before else sent):
            got[part] = lax.ppermute(x, "vv", [(i, i ^ part[0]) for i in range(vv)])

    made = []

    def multiply(parts, *before):
        made.append(product(after([got[part] for part in parts], *made[-1:], *before), integrals))
        return made[-1]

    def hop(x, j, bit):
        pairs = [
            (a * oo + b, a * oo + (b ^ bit))
            for a in range(vv)
            for b in range(oo)
            if ((a // ratio) ^ b ^ j) % (2 * bit) == bit
        ]
        return lax.ppermute(x, ("vv", "oo"), pairs)

    def inner(each):
        for part in each:
            for bit in bits:
                each[part] = each[part] + hop(each[part], part[0] // ratio, bit)
        return each

    def outer(each):
        return {part: x + hop(x, part[0] // ratio, top) for part, x in each.items()}

    def fold(x):
        for bit in bits:
            mine = (offset // bit) % 2 == 1
            n = x[0].shape[0]
            sent = jnp.concatenate([jnp.where(mine, one, two) for one, two in zip(x[::2], x[1::2])])
            came = lax.ppermute(sent, "oo", [(i, i ^ bit) for i in range(oo)])
            x = [jnp.where(mine, two, one) + came[i * n : (i + 1) * n] for i, (one, two) in enumerate(zip(x[::2], x[1::2]))]
        return x[0]

    def place(out, x, part, mine):
        row = ((v ^ part[0]) % ratio) * columns + part[1]
        return lax.dynamic_update_slice(out, jnp.where(mine, x, lax.dynamic_slice(out, (row, 0), x.shape)), (row, 0))

    fetch(first)
    fetch(second, *[got[part] for part in first[:quarter]])
    middle = [got[part] for part in second]
    fetch(third, *middle)
    near = []
    for j in range(top):
        arrived = [got[part] for part in first[:quarter]]
        near.append(multiply([whole[mask] for mask in range(j * ratio, (j + 1) * ratio)], *arrived))
    early = {}
    for j in range(top, top + top // 2):
        early[j * ratio, 0, ratio * columns] = multiply([whole[mask] for mask in range(j * ratio, (j + 1) * ratio)])
    near = fold(near)
    early = inner(dict(zip(early, after(list(early.values()), *middle))))
    pairs = [(a * oo + b, a * oo + (b ^ top)) for a in range(vv) for b in range(oo) if ((a // ratio) ^ b) & top]
    near = near + lax.ppermute(near, ("vv", "oo"), pairs)
    early = outer(early)
    late, before = {}, []
    for part in [*second, *third]:
        if part == third[0]:
            before += [near, *early.values()]
        sums = inner({part: multiply([part], *before)})
        before = list(sums.values())
        late.update(outer(sums))

    out = jnp.zeros((ratio * columns, rows), jnp.float32)
    for low in range(ratio):
        rows_of = slice(low * columns, (low + 1) * columns)
        out = place(out, near[rows_of], whole[low], offset < top)
        for part, x in early.items():
            out = place(out, x[rows_of], whole[part[0] + low], offset == part[0] // ratio)
    for part, x in late.items():
        out = place(out, x, part, offset == part[0] // ratio)
    return out.T


def solution(mesh):
    vv, oo = mesh.shape["vv"], mesh.shape["oo"]
    in_specs = (P("vv", "oo"), P(None, "oo", "vv"), P())
    return jax.shard_map(
        lambda *a: local(vv, oo, *a), mesh=mesh, in_specs=in_specs, out_specs=P("vv", "oo"), check_vma=False
    )
```

```python
import math

import jax
import jax.numpy as jnp
from jax import lax
from jax.experimental import pallas as pl
from jax.experimental.pallas import tpu as pltpu
from jax.sharding import PartitionSpec as P

BLOCK = 512
SHORT = 10
TILE = 16
LINK_SHARE = 64
CUT = 80


def cut_kernel(owner, me, *refs):
    n = len(refs) // 2
    for block, out in zip(refs[:n], refs[n:]):
        out[...] = block[0]


def cut(parts, owner, me, blocks):
    depth = blocks.shape[2]
    _, start, width = parts[0]
    step = math.gcd(math.gcd(start, width), CUT)
    return pl.pallas_call(
        cut_kernel,
        grid_spec=pltpu.PrefetchScalarGridSpec(
            num_scalar_prefetch=2,
            grid=(width // step,),
            in_specs=[
                pl.BlockSpec((1, step, depth), lambda i, owner, me, mask=mask: (owner[me[0] ^ mask], start // step + i, 0))
                for mask, _, _ in parts
            ],
            out_specs=[pl.BlockSpec((step, depth), lambda i, owner, me: (i, 0))] * len(parts),
        ),
        out_shape=[jax.ShapeDtypeStruct((width, depth), blocks.dtype)] * len(parts),
        cost_estimate=pl.CostEstimate(flops=0, bytes_accessed=4 * depth * width * len(parts), transcendentals=0),
        compiler_params=pltpu.CompilerParams(vmem_limit_bytes=56 * 2**20),
    )(owner, me, *[blocks] * len(parts))


def product_kernel(*refs):
    *pieces, rows, out, held = refs

    @pl.when(pl.program_id(0) == 0)
    def _():
        at = 0
        for piece in pieces:
            held[at : at + piece.shape[0], :] = piece[...]
            at += piece.shape[0]

    out[...] = lax.dot_general(held[...], rows[...], (((1,), (1,)), ((), ())), preferred_element_type=jnp.float32)


def product(pieces, integrals):
    depth, rows = pieces[0].shape[1], integrals.shape[0]
    n = sum(piece.shape[0] for piece in pieces)
    block = min(BLOCK, rows)
    return pl.pallas_call(
        product_kernel,
        grid=(rows // block,),
        in_specs=[pl.BlockSpec(piece.shape, lambda i: (0, 0)) for piece in pieces]
        + [pl.BlockSpec((block, depth), lambda i: (i, 0))],
        out_specs=pl.BlockSpec((n, block), lambda i: (0, i)),
        out_shape=jax.ShapeDtypeStruct((n, rows), jnp.float32),
        scratch_shapes=[pltpu.VMEM((n, depth), pieces[0].dtype)],
        cost_estimate=pl.CostEstimate(
            flops=2 * n * depth * rows // LINK_SHARE,
            bytes_accessed=(2 * (n + rows) * depth + 4 * n * rows) // LINK_SHARE,
            transcendentals=0,
        ),
        compiler_params=pltpu.CompilerParams(vmem_limit_bytes=48 * 2**20),
    )(*pieces, integrals)


def after(xs, *others):
    return list(lax.optimization_barrier((*xs, *others))[: len(xs)])


def local(vv, oo, integrals, t2, block_owner):
    v, o = lax.axis_index("vv"), lax.axis_index("oo")
    blocks = jnp.swapaxes(t2, 1, 2)
    columns, rows = blocks.shape[1], integrals.shape[0]
    ratio = vv // oo
    offset = (v // ratio) ^ o
    me = v.reshape(1)
    half, quarter = vv // 2, vv // 4

    top = oo // 2
    bits = [1 << k for k in range(top.bit_length() - 1)]
    whole = {mask: (mask, 0, columns) for mask in range(vv)}
    first = [whole[mask] for mask in [*range(half, half + quarter), *range(1, half)]]
    short = max(columns // SHORT // TILE, 1) * TILE
    cuts = [0, columns - short, columns]
    third = [(vv - 1, one, two - one) for one, two in zip(cuts, cuts[1:])]
    second = [whole[mask] for mask in range(half + quarter, vv - 1)]
    ready = {}
    for some in (first[:quarter], [*first[quarter:], whole[0], *second, whole[vv - 1]]):
        ready.update(zip(some, cut(some, block_owner, me, blocks)))
    got = {whole[0]: ready[whole[0]]}
    for part in third:
        ready[part] = ready[whole[vv - 1]][part[1] : part[1] + part[2]]

    def fetch(parts, *before):
        sent = [ready[part] for part in parts]
        for part, x in zip(parts, after(sent, *before) if before else sent):
            got[part] = lax.ppermute(x, "vv", [(i, i ^ part[0]) for i in range(vv)])

    made = []

    def multiply(parts, *before):
        made.append(product(after([got[part] for part in parts], *made[-1:], *before), integrals))
        return made[-1]

    def hop(x, j, bit):
        pairs = [
            (a * oo + b, a * oo + (b ^ bit))
            for a in range(vv)
            for b in range(oo)
            if ((a // ratio) ^ b ^ j) % (2 * bit) == bit
        ]
        return lax.ppermute(x, ("vv", "oo"), pairs)

    def inner(each):
        for part in each:
            for bit in bits:
                each[part] = each[part] + hop(each[part], part[0] // ratio, bit)
        return each

    def outer(each):
        return {part: x + hop(x, part[0] // ratio, top) for part, x in each.items()}

    def fold(x):
        for bit in bits:
            mine = (offset // bit) % 2 == 1
            n = x[0].shape[0]
            sent = jnp.concatenate([jnp.where(mine, one, two) for one, two in zip(x[::2], x[1::2])])
            came = lax.ppermute(sent, "oo", [(i, i ^ bit) for i in range(oo)])
            x = [jnp.where(mine, two, one) + came[i * n : (i + 1) * n] for i, (one, two) in enumerate(zip(x[::2], x[1::2]))]
        return x[0]

    def place(out, x, part, mine):
        row = ((v ^ part[0]) % ratio) * columns + part[1]
        return lax.dynamic_update_slice(out, jnp.where(mine, x, lax.dynamic_slice(out, (row, 0), x.shape)), (row, 0))

    fetch(first)
    fetch(second, *[got[part] for part in first[:quarter]])
    middle = [got[part] for part in second]
    fetch(third, *middle)
    near = []
    for j in range(top):
        arrived = [got[part] for part in first[:quarter]]
        near.append(multiply([whole[mask] for mask in range(j * ratio, (j + 1) * ratio)], *arrived))
    early = {}
    for j in range(top, top + top // 2):
        early[j * ratio, 0, ratio * columns] = multiply([whole[mask] for mask in range(j * ratio, (j + 1) * ratio)])
    near = fold(near)
    early = inner(dict(zip(early, after(list(early.values()), *middle))))
    pairs = [(a * oo + b, a * oo + (b ^ top)) for a in range(vv) for b in range(oo) if ((a // ratio) ^ b) & top]
    near = near + lax.ppermute(near, ("vv", "oo"), pairs)
    early = outer(early)
    late, before = {}, []
    for part in [*second, *third]:
        if part == third[0]:
            before += [near, *early.values()]
        if part == third[-1]:
            before += [late[done] for done in second]
        sums = inner({part: multiply([part], *before)})
        before = list(sums.values())
        late.update(outer(sums))

    out = jnp.zeros((ratio * columns, rows), jnp.float32)
    for low in range(ratio):
        rows_of = slice(low * columns, (low + 1) * columns)
        out = place(out, near[rows_of], whole[low], offset < top)
        for part, x in early.items():
            out = place(out, x[rows_of], whole[part[0] + low], offset == part[0] // ratio)
    for part, x in late.items():
        out = place(out, x, part, offset == part[0] // ratio)
    return out.T


def solution(mesh):
    vv, oo = mesh.shape["vv"], mesh.shape["oo"]
    in_specs = (P("vv", "oo"), P(None, "oo", "vv"), P())
    return jax.shard_map(
        lambda *a: local(vv, oo, *a), mesh=mesh, in_specs=in_specs, out_specs=P("vv", "oo"), check_vma=False
    )
```

```python
import math

import jax
import jax.numpy as jnp
from jax import lax
from jax.experimental import pallas as pl
from jax.experimental.pallas import tpu as pltpu
from jax.sharding import PartitionSpec as P

BLOCK = 512
SHORT = 10
TILE = 16
LINK_SHARE = 64
CUT = 80


def cut_kernel(owner, me, *refs):
    n = len(refs) // 2
    for block, out in zip(refs[:n], refs[n:]):
        out[...] = block[0]


def cut(parts, owner, me, blocks):
    depth = blocks.shape[2]
    _, start, width = parts[0]
    step = math.gcd(math.gcd(start, width), CUT)
    return pl.pallas_call(
        cut_kernel,
        grid_spec=pltpu.PrefetchScalarGridSpec(
            num_scalar_prefetch=2,
            grid=(width // step,),
            in_specs=[
                pl.BlockSpec((1, step, depth), lambda i, owner, me, mask=mask: (owner[me[0] ^ mask], start // step + i, 0))
                for mask, _, _ in parts
            ],
            out_specs=[pl.BlockSpec((step, depth), lambda i, owner, me: (i, 0))] * len(parts),
        ),
        out_shape=[jax.ShapeDtypeStruct((width, depth), blocks.dtype)] * len(parts),
        cost_estimate=pl.CostEstimate(flops=0, bytes_accessed=4 * depth * width * len(parts), transcendentals=0),
        compiler_params=pltpu.CompilerParams(vmem_limit_bytes=56 * 2**20),
    )(owner, me, *[blocks] * len(parts))


def product_kernel(*refs):
    *pieces, rows, out, held = refs

    @pl.when(pl.program_id(0) == 0)
    def _():
        at = 0
        for piece in pieces:
            held[at : at + piece.shape[0], :] = piece[...]
            at += piece.shape[0]

    out[...] = lax.dot_general(held[...], rows[...], (((1,), (1,)), ((), ())), preferred_element_type=jnp.float32)


def product(pieces, integrals):
    depth, rows = pieces[0].shape[1], integrals.shape[0]
    n = sum(piece.shape[0] for piece in pieces)
    block = min(BLOCK, rows)
    return pl.pallas_call(
        product_kernel,
        grid=(rows // block,),
        in_specs=[pl.BlockSpec(piece.shape, lambda i: (0, 0)) for piece in pieces]
        + [pl.BlockSpec((block, depth), lambda i: (i, 0))],
        out_specs=pl.BlockSpec((n, block), lambda i: (0, i)),
        out_shape=jax.ShapeDtypeStruct((n, rows), jnp.float32),
        scratch_shapes=[pltpu.VMEM((n, depth), pieces[0].dtype)],
        cost_estimate=pl.CostEstimate(
            flops=2 * n * depth * rows // LINK_SHARE,
            bytes_accessed=(2 * (n + rows) * depth + 4 * n * rows) // LINK_SHARE,
            transcendentals=0,
        ),
        compiler_params=pltpu.CompilerParams(vmem_limit_bytes=48 * 2**20),
    )(*pieces, integrals)


def after(xs, *others):
    return list(lax.optimization_barrier((*xs, *others))[: len(xs)])


def local(vv, oo, integrals, t2, block_owner):
    v, o = lax.axis_index("vv"), lax.axis_index("oo")
    blocks = jnp.swapaxes(t2, 1, 2)
    columns, rows = blocks.shape[1], integrals.shape[0]
    ratio = vv // oo
    offset = (v // ratio) ^ o
    me = v.reshape(1)
    half, quarter = vv // 2, vv // 4

    top = oo // 2
    bits = [1 << k for k in range(top.bit_length() - 1)]
    whole = {mask: (mask, 0, columns) for mask in range(vv)}
    first = [whole[mask] for mask in [*range(half, half + quarter), *range(1, half)]]
    short = max(columns // SHORT // TILE, 1) * TILE
    cuts = [0, short, columns]
    third = [(vv - 1, one, two - one) for one, two in zip(cuts, cuts[1:])]
    second = [whole[mask] for mask in range(half + quarter, vv - 1)]
    ready = {}
    for some in (first[:quarter], [*first[quarter:], whole[0], *second, whole[vv - 1]]):
        ready.update(zip(some, cut(some, block_owner, me, blocks)))
    got = {whole[0]: ready[whole[0]]}
    for part in third:
        ready[part] = ready[whole[vv - 1]][part[1] : part[1] + part[2]]

    def fetch(parts, *before):
        sent = [ready[part] for part in parts]
        for part, x in zip(parts, after(sent, *before) if before else sent):
            got[part] = lax.ppermute(x, "vv", [(i, i ^ part[0]) for i in range(vv)])

    made = []

    def multiply(parts, *before):
        made.append(product(after([got[part] for part in parts], *made[-1:], *before), integrals))
        return made[-1]

    def hop(x, j, bit):
        pairs = [
            (a * oo + b, a * oo + (b ^ bit))
            for a in range(vv)
            for b in range(oo)
            if ((a // ratio) ^ b ^ j) % (2 * bit) == bit
        ]
        return lax.ppermute(x, ("vv", "oo"), pairs)

    def inner(each):
        for part in each:
            for bit in bits:
                each[part] = each[part] + hop(each[part], part[0] // ratio, bit)
        return each

    def outer(each):
        return {part: x + hop(x, part[0] // ratio, top) for part, x in each.items()}

    def fold(x):
        for bit in bits:
            mine = (offset // bit) % 2 == 1
            n = x[0].shape[0]
            sent = jnp.concatenate([jnp.where(mine, one, two) for one, two in zip(x[::2], x[1::2])])
            came = lax.ppermute(sent, "oo", [(i, i ^ bit) for i in range(oo)])
            x = [jnp.where(mine, two, one) + came[i * n : (i + 1) * n] for i, (one, two) in enumerate(zip(x[::2], x[1::2]))]
        return x[0]

    def place(out, x, part, mine):
        row = ((v ^ part[0]) % ratio) * columns + part[1]
        return lax.dynamic_update_slice(out, jnp.where(mine, x, lax.dynamic_slice(out, (row, 0), x.shape)), (row, 0))

    fetch(first)
    fetch(second, *[got[part] for part in first[:quarter]])
    middle = [got[part] for part in second]
    fetch(third, *middle)
    near = []
    for j in range(top):
        arrived = [got[part] for part in first[:quarter]]
        near.append(multiply([whole[mask] for mask in range(j * ratio, (j + 1) * ratio)], *arrived))
    early = {}
    for j in range(top, top + top // 2):
        early[j * ratio, 0, ratio * columns] = multiply([whole[mask] for mask in range(j * ratio, (j + 1) * ratio)])
    near = fold(near)
    early = inner(dict(zip(early, after(list(early.values()), *middle))))
    pairs = [(a * oo + b, a * oo + (b ^ top)) for a in range(vv) for b in range(oo) if ((a // ratio) ^ b) & top]
    near = near + lax.ppermute(near, ("vv", "oo"), pairs)
    early = outer(early)
    late, before = {}, []
    for part in [*second, *third]:
        if part == third[0]:
            before += [near, *early.values()]
        sums = inner({part: multiply([part], *before)})
        before = list(sums.values())
        late.update(outer(sums))

    out = jnp.zeros((ratio * columns, rows), jnp.float32)
    for low in range(ratio):
        rows_of = slice(low * columns, (low + 1) * columns)
        out = place(out, near[rows_of], whole[low], offset < top)
        for part, x in early.items():
            out = place(out, x[rows_of], whole[part[0] + low], offset == part[0] // ratio)
    for part, x in late.items():
        out = place(out, x, part, offset == part[0] // ratio)
    return out.T


def solution(mesh):
    vv, oo = mesh.shape["vv"], mesh.shape["oo"]
    in_specs = (P("vv", "oo"), P(None, "oo", "vv"), P())
    return jax.shard_map(
        lambda *a: local(vv, oo, *a), mesh=mesh, in_specs=in_specs, out_specs=P("vv", "oo"), check_vma=False
    )
```
